128 devices in a mesh: dp: 8 (over y, core), ctx: 16 (over x, z).
Axes of the slice: x: 4, y: 4, z: 4, core: 2. Of those that a mesh axis runs over, the one named last changes fastest.
Arguments:
- features: bfloat16 [8, 2048, 4096], P('dp', 'ctx'), may hold values from -6 to 6
- queries: bfloat16 [8, 2048, 4096], P('dp', 'ctx'), may hold values from -100 to 100
- keys: bfloat16 [8, 2048, 1024], P('dp', 'ctx'), may hold values from -4 to 4
- values: bfloat16 [8, 2048, 1024], P('dp', 'ctx'), may hold values from -6 to 6
- grad_out: bfloat16 [8, 2048, 4096], P('dp', 'ctx'), may hold values from -6 to 6
- lengths: int32 [8], P('dp'), may hold values from 512 to 2048, as said below
- placement: int32 [8, 16], P('dp'), may hold values from 0 to 15, as said below
- query_down: bfloat16 [4096, 16], replicated, may hold values from -0.09375 to 0.09375
- query_up: bfloat16 [16, 4096], replicated, may hold values from -1.5 to 1.5
- value_down: bfloat16 [4096, 16], replicated, may hold values from -0.09375 to 0.09375
- value_up: bfloat16 [16, 1024], replicated, may hold values from -1.5 to 1.5
Outputs:
- grad_query: bfloat16 [8, 2048, 4096], P('dp', 'ctx')
- grad_key: bfloat16 [8, 2048, 1024], P('dp', 'ctx')
- grad_value: bfloat16 [8, 2048, 1024], P('dp', 'ctx')
- query_down_gradient: float32 [4096, 16], replicated
- query_up_gradient: float32 [16, 4096], replicated
- value_down_gradient: float32 [4096, 16], replicated
- value_up_gradient: float32 [16, 1024], replicated
The draws below stay inside these ranges and needn't reach their ends.
Inputs may be any that keep to these rules, and one draw needn't show every extreme that they name: `lengths`: some chain has all 2048 positions live. `placement`: each row is a permutation of the tiles of a chain.
All inputs are finite; a program needn't handle non-finite values.
Results may differ from the reference program's by a relative error of at most 0.01.
Values may be sent and summed in bfloat16 or wider, within the bound.
No kernel may reach another device: no remote copies, remote signals or barrier semaphores. Data moves between devices by JAX's collectives and lax.ppermute only.
A program may use at most 192 MiB of HBM per device.

```python
import math
import jax
import jax.numpy as jnp
from jax import lax

D = 4096
H = 32
KVH = 8
DH = 128
R = 16
S_DEV = 128
CHAINS = 8
TILES = 16
WINDOW = 2048


def shared_keys(key):
    base = jnp.clip(jax.random.normal(key, (CHAINS, WINDOW, KVH * DH), jnp.float32), -4.0, 4.0)
    return base


def draw_keys(key, part):
    base = shared_keys(key)
    return base.astype(jnp.bfloat16)


def draw_queries(key, part):
    key = jax.random.fold_in(key, 3)
    own = jnp.clip(jax.random.normal(key, (CHAINS, WINDOW, H * DH), jnp.float32), -4.0, 4.0)
    return own.astype(jnp.bfloat16)


def draw_lengths(key, part):
    key = jax.random.fold_in(key, 7)
    drawn = jax.random.randint(key, (CHAINS,), WINDOW // 4, WINDOW + 1)
    chosen = jax.random.randint(jax.random.fold_in(key, 1), (), 0, CHAINS)
    return jnp.where(jnp.arange(CHAINS) == chosen, WINDOW, drawn).astype(jnp.int32)


def draw_placement(key, part):
    key = jax.random.fold_in(key, 11)
    several = jax.random.split(key, CHAINS)
    return jax.vmap(lambda single: jax.random.permutation(single, TILES))(several).astype(jnp.int32)


def block_levels(stream_key, dims, cuts, low, largest):
    loudness, own = 1.0, jax.random.fold_in(stream_key, 6)
    for dim, blocks in cuts:
        draws = jnp.exp(jax.random.uniform(jax.random.fold_in(own, dim), (blocks,), jnp.float32, low / len(cuts), largest / len(cuts)))
        loudness = loudness * jnp.repeat(draws, dims[dim] // blocks).reshape([-1 if axis == dim else 1 for axis in range(len(dims))])
    return loudness


def scatter_about(key, dims, deviation, bound, cuts=(), kind=jnp.bfloat16):
    gain = block_levels(key, dims, cuts, -0.22, 0.18) if cuts else 1.0
    array = jax.random.normal(key, dims, jnp.float32) * deviation * gain
    return jnp.minimum(jnp.maximum(array, -bound), bound).astype(kind)


def setup_inputs(seed: int = 0) -> dict:
    seeds = jax.random.split(jax.random.key(seed), 12)
    return {
        "features": scatter_about(seeds[0], (CHAINS, WINDOW, D), 1.0, 6.0, ((0, 8), (1, 16))),
        "queries": draw_queries(jax.random.fold_in(seeds[11], 71), 0),
        "keys": draw_keys(jax.random.fold_in(seeds[11], 71), 0),
        "values": scatter_about(seeds[3], (CHAINS, WINDOW, KVH * DH), 1.0, 6.0, ((0, 8), (1, 16))),
        "grad_out": scatter_about(seeds[4], (CHAINS, WINDOW, H * DH), 1.0, 6.0, ((0, 8), (1, 16))),
        "lengths": draw_lengths(jax.random.fold_in(seeds[11], 71), 0),
        "placement": draw_placement(jax.random.fold_in(seeds[11], 71), 0),
        "query_down": scatter_about(seeds[7], (D, R), D ** -0.5, 0.09375),
        "query_up": scatter_about(seeds[8], (R, H * DH), R ** -0.5, 1.5),
        "value_down": scatter_about(seeds[9], (D, R), D ** -0.5, 0.09375),
        "value_up": scatter_about(seeds[10], (R, KVH * DH), R ** -0.5, 1.5),
    }


ADAPTER_SCALING = 2.0

def row_positions(place_row):
    rows = jnp.arange(S_DEV * TILES, dtype=jnp.int32)
    return place_row[rows // S_DEV] * S_DEV + rows % S_DEV

def unrotate(gradient, position):
    half = DH // 2
    freq = jnp.exp(-jnp.arange(half, dtype=jnp.float32) * (math.log(500000.0) / half))
    angle = position.astype(jnp.float32)[:, None] * freq[None, :]
    cosine = jnp.cos(angle)[:, None, :]
    sine = jnp.sin(angle)[:, None, :]
    shaped = gradient.reshape(gradient.shape[0], H, DH)
    first = shaped[..., :half]
    second = shaped[..., half:]
    joined = jnp.concatenate([first * cosine + second * sine, second * cosine - first * sine], -1)
    return joined.reshape(gradient.shape[0], H * DH)

def group_grads(query, key_col, value_col, out_grad, allowed):
    scale = 1.0 / math.sqrt(DH)
    logits = jnp.einsum('qgd,kd->gqk', query.astype(jnp.float32), key_col.astype(jnp.float32)) * scale
    logits = jnp.where(allowed[None], logits, -jnp.inf)
    peak = lax.optimization_barrier(jnp.max(logits, -1, keepdims=True))
    lse = peak + jnp.log(lax.optimization_barrier(jnp.sum(jnp.exp(logits - peak), -1, keepdims=True)))
    prob = jnp.exp(logits - lse)
    prob_half = prob.astype(jnp.bfloat16)
    attended = jnp.einsum('gqk,kd->qgd', prob_half.astype(jnp.float32), value_col.astype(jnp.float32))
    delta = lax.optimization_barrier(jnp.sum(out_grad.astype(jnp.float32) * attended, -1))
    grad_prob = jnp.einsum('qgd,kd->gqk', out_grad.astype(jnp.float32), value_col.astype(jnp.float32))
    grad_logit = (prob * (grad_prob - delta.T[:, :, None])).astype(jnp.bfloat16)
    grad_q = jnp.einsum('gqk,kd->qgd', grad_logit.astype(jnp.float32), key_col.astype(jnp.float32)) * scale
    grad_k = jnp.einsum('gqk,qgd->kd', grad_logit.astype(jnp.float32), query.astype(jnp.float32)) * scale
    grad_v = jnp.einsum('gqk,qgd->kd', prob_half.astype(jnp.float32), out_grad.astype(jnp.float32))
    return (grad_q, grad_k, grad_v)

def reference(features, queries, keys, values, grad_out, lengths, placement, query_down, query_up, value_down, value_up):
    groups = H // KVH
    width = S_DEV * TILES

    def one_chain(item):
        chain_q, chain_k, chain_v, chain_g, length, place_row = item
        position = row_positions(place_row)
        allowed = (position[None, :] <= position[:, None]) & (position[None, :] < length)
        live = position < length
        masked_out = jnp.where(live[:, None], chain_g, jnp.zeros((), jnp.bfloat16))
        heads_q = chain_q.reshape(width, KVH, groups, DH).transpose(1, 0, 2, 3)
        heads_k = chain_k.reshape(width, KVH, DH).transpose(1, 0, 2)
        heads_v = chain_v.reshape(width, KVH, DH).transpose(1, 0, 2)
        heads_g = masked_out.reshape(width, KVH, groups, DH).transpose(1, 0, 2, 3)
        grad_q, grad_k, grad_v = lax.map(lambda item2: group_grads(item2[0], item2[1], item2[2], item2[3], allowed), (heads_q, heads_k, heads_v, heads_g))
        grad_q = grad_q.transpose(1, 0, 2, 3).reshape(width, H * DH)
        grad_k = grad_k.transpose(1, 0, 2).reshape(width, KVH * DH)
        grad_v = grad_v.transpose(1, 0, 2).reshape(width, KVH * DH)
        return (grad_q, grad_k, grad_v)
    grad_q, grad_k, grad_v = lax.map(one_chain, (queries, keys, values, grad_out, lengths, placement))
    grad_query = grad_q.astype(jnp.bfloat16)
    grad_key = grad_k.astype(jnp.bfloat16)
    grad_value = grad_v.astype(jnp.bfloat16)
    position_all = jax.vmap(row_positions)(placement).reshape(-1)
    flat_rows = CHAINS * width
    query_before_rotary = unrotate(grad_q.reshape(flat_rows, H * DH), position_all).astype(jnp.bfloat16)
    value_flattened = grad_value.reshape(flat_rows, KVH * DH)
    hidden_features = features.reshape(flat_rows, D)
    query_low_rank = jnp.dot(hidden_features, query_down, preferred_element_type=jnp.float32).astype(jnp.bfloat16)
    value_low_rank = jnp.dot(hidden_features, value_down, preferred_element_type=jnp.float32).astype(jnp.bfloat16)
    query_inner_product = jnp.dot(query_before_rotary, query_up.T, preferred_element_type=jnp.float32).astype(jnp.bfloat16)
    value_inner_product = jnp.dot(value_flattened, value_up.T, preferred_element_type=jnp.float32).astype(jnp.bfloat16)
    query_up_gradient = ADAPTER_SCALING * jnp.dot(query_low_rank.T, query_before_rotary, preferred_element_type=jnp.float32)
    value_up_gradient = ADAPTER_SCALING * jnp.dot(value_low_rank.T, value_flattened, preferred_element_type=jnp.float32)
    query_down_gradient = ADAPTER_SCALING * jnp.dot(hidden_features.T, query_inner_product, preferred_element_type=jnp.float32)
    value_down_gradient = ADAPTER_SCALING * jnp.dot(hidden_features.T, value_inner_product, preferred_element_type=jnp.float32)
    return (grad_query, grad_key, grad_value, query_down_gradient, query_up_gradient, value_down_gradient, value_up_gradient)
```

```python
import math

import jax
import jax.numpy as jnp
import numpy as np
from jax import lax
from jax.experimental import pallas as pl
from jax.experimental.pallas import tpu as pltpu
from jax.sharding import PartitionSpec as P

D = 4096
H = 32
KVH = 8
DH = 128
R = 16
TILE = 128
TILES = 16
WINDOW = TILE * TILES
DEVICES = 128
DP = 8
SCALE = 1.0 / math.sqrt(DH)
LOG2E = math.log2(math.e)
ADAPTER_SCALING = 2.0
FAR_BELOW = -1e30
IN_ROWS = 6 * TILE + 2 * R
OUT_ROWS = 4 * TILE + 2 * R
QB = 256
BLOCKS = WINDOW // QB

F32 = jnp.float32
BF16 = jnp.bfloat16
VMEM = pl.BlockSpec(memory_space=pltpu.VMEM)
SMEM = pl.BlockSpec(memory_space=pltpu.SMEM)


def nt(a, b):
    return lax.dot_general(a, b, (((1,), (1,)), ((), ())), preferred_element_type=F32)


def nn(a, b):
    return lax.dot_general(a, b, (((1,), (0,)), ((), ())), preferred_element_type=F32)


def params(mebibytes):
    return pltpu.CompilerParams(vmem_limit_bytes=mebibytes * 1024 * 1024)


def pack_kernel(info, features, queries, keys, values, grad_out, q_down, v_down, out):
    low_q = nt(q_down[...], features[...]).astype(BF16)
    low_v = nt(v_down[...], features[...]).astype(BF16)
    for j in range(TILES):
        h = j // 2
        out[j, 0:128] = queries[:, j * 256 : j * 256 + 128]
        out[j, 128:256] = queries[:, j * 256 + 128 : j * 256 + 256]
        out[j, 256:384] = grad_out[:, j * 256 : j * 256 + 128]
        out[j, 384:512] = grad_out[:, j * 256 + 128 : j * 256 + 256]
        out[j, 512:640] = keys[:, h * 128 : h * 128 + 128]
        out[j, 640:768] = values[:, h * 128 : h * 128 + 128]
        out[j, 768:784] = low_q
        out[j, 784:800] = low_v


def pack(info, features, queries, keys, values, grad_out, q_down, v_down):
    return pl.pallas_call(
        pack_kernel,
        out_shape=jax.ShapeDtypeStruct((TILES, IN_ROWS, 128), BF16),
        in_specs=[SMEM] + [VMEM] * 7,
        out_specs=VMEM,
        compiler_params=params(56),
        name="pack",
    )(info, features, queries, keys, values, grad_out, q_down, v_down)


def attention_kernel(
    place,
    info,
    recv,
    q_up,
    v_up,
    cos_t,
    sin_t,
    out,
    up_out,
    qs,
    gs,
    ks,
    vs,
    kt,
    low,
    s_all,
    dp_all,
    dk,
    dv,
    inner,
    upg,
    inv,
):
    here = info[0]
    length = info[1]
    rows = lax.broadcasted_iota(jnp.int32, (TILE, 128), 0)

    def arrange(t, _):
        p = place[t]
        inv[p] = t
        block = p // 2
        offset = pl.multiple_of((p % 2) * TILE, TILE)
        at = pl.ds(pl.multiple_of(p * TILE, TILE), TILE)
        live = rows + p * TILE < length
        for h in range(2):
            to = pl.ds(pl.multiple_of(h * QB + offset, TILE), TILE)
            qs[block, to] = recv[t, h * 128 : h * 128 + 128]
            grad = recv[t, 256 + h * 128 : 384 + h * 128].astype(F32)
            gs[block, to] = jnp.where(live, grad, 0.0).astype(BF16)
        key = recv[t, 512:640]
        ks[at] = key
        vs[at] = recv[t, 640:768]
        kt[:, at] = key.astype(F32).T.astype(BF16)
        low[:, at] = recv[t, 768:800]
        return 0

    for t in range(TILES):
        arrange(t, 0)
    dk[...] = jnp.zeros_like(dk)
    dv[...] = jnp.zeros_like(dv)
    inner[...] = jnp.zeros_like(inner)
    upg[...] = jnp.zeros_like(upg)
    q_up_here = [
        q_up[:, pl.ds(pl.multiple_of(here * 256 + h * 128, 128), 128)] for h in range(2)
    ]
    v_up_here = v_up[:, pl.ds(pl.multiple_of((here // 2) * 128, 128), 128)]
    base = SCALE * LOG2E

    def block_step(i, _):
        @pl.when(i * QB < length)
        def _():
            query = qs[i]
            grad = gs[i]

            def first(j, carry, diagonal=False):
                peak, total, weighted = carry
                at = pl.ds(pl.multiple_of(j * QB, QB), QB)
                s = nt(ks[at], query)
                dp = nt(vs[at], grad)
                if diagonal:
                    ki = lax.broadcasted_iota(jnp.int32, (QB, 2 * QB), 0)
                    qi = lax.broadcasted_iota(jnp.int32, (QB, 2 * QB), 1) & (QB - 1)
                    s = jnp.where(ki <= qi, s, FAR_BELOW)
                s_all[at] = s
                dp_all[at] = dp
                new = jnp.maximum(peak, jnp.max(s, 0, keepdims=True))
                e = jnp.exp2(s * base - new * base)
                alpha = jnp.exp2((peak - new) * base)
                total = total * alpha + jnp.sum(e, 0, keepdims=True)
                weighted = weighted * alpha + jnp.sum(e * dp, 0, keepdims=True)
                return new, total, weighted

            zero = jnp.zeros((1, 2 * QB), F32)
            carry = (jnp.full((1, 2 * QB), FAR_BELOW, F32), zero, zero)
            for j in range(i):
                carry = first(j, carry)
            peak, total, weighted = first(i, carry, True)
            lse = peak * base + jnp.log2(total)
            delta = weighted / total

            def second(j, dq):
                at = pl.ds(pl.multiple_of(j * QB, QB), QB)
                prob = jnp.exp2(s_all[at] * base - lse)
                grad_logit = (prob * (dp_all[at] - delta)).astype(BF16)
                dv[at] += nn(prob.astype(BF16), grad)
                dk[at] += nn(grad_logit, query)
                return dq + nn(kt[:, at], grad_logit)

            dq = jnp.zeros((128, 2 * QB), F32)
            for j in range(i + 1):
                dq = second(j, dq)
            dq = dq * SCALE
            span = pl.ds(pl.multiple_of(i * QB, QB), QB)
            cosine = cos_t[:, span]
            sine = sin_t[:, span]
            low_q = low[0:R, span]
            inner_q = jnp.zeros((R, QB), F32)
            for h in range(2):
                a = dq[0:64, h * QB : h * QB + QB]
                b = dq[64:128, h * QB : h * QB + QB]
                pre = jnp.concatenate([a * cosine + b * sine, b * cosine - a * sine], 0)
                pre = pre.astype(BF16)
                inner_q = inner_q + nn(q_up_here[h], pre)
                upg[h * R : h * R + R] += nt(low_q, pre)
                back = dq[:, h * QB : h * QB + QB].T.astype(BF16)
                for half in range(2):
                    out[inv[2 * i + half], h * 128 : h * 128 + 128] = back[
                        half * TILE : half * TILE + TILE
                    ]
            inner[0:R, span] = inner_q

        @pl.when(i * QB >= length)
        def _():
            for half in range(2):
                out[inv[2 * i + half], 0:256] = jnp.zeros((256, 128), BF16)

        return 0

    for i in range(BLOCKS):
        block_step(i, 0)

    grad_value = dv[...].astype(BF16)
    inner[R : 2 * R] = nt(v_up_here, grad_value)
    upg[2 * R : 3 * R] = nn(low[R : 2 * R], grad_value)
    for p in range(TILES):
        at = slice(p * TILE, p * TILE + TILE)
        t = inv[p]
        out[t, 256:384] = (dk[at] * SCALE).astype(BF16)
        out[t, 384:512] = dv[at].astype(BF16)
        out[t, 512:544] = inner[:, at].astype(BF16)
    total = upg[...] * ADAPTER_SCALING
    for c in range(DP):
        up_out[c] = total[c * 8 : c * 8 + 8]


def rotary_tables():
    half = DH // 2
    freq = np.exp(-np.arange(half, dtype=np.float32) * np.float32(math.log(500000.0) / half))
    angle = freq.astype(np.float32)[:, None] * np.arange(WINDOW, dtype=np.float32)[None, :]
    return np.cos(angle).astype(np.float32), np.sin(angle).astype(np.float32)


def attention(place, info, recv, q_up, v_up):
    cos_t, sin_t = rotary_tables()
    return pl.pallas_call(
        attention_kernel,
        out_shape=(
            jax.ShapeDtypeStruct((TILES, OUT_ROWS, 128), BF16),
            jax.ShapeDtypeStruct((DP, 8, 128), F32),
        ),
        in_specs=[SMEM, SMEM] + [VMEM] * 5,
        out_specs=(VMEM, VMEM),
        scratch_shapes=[
            pltpu.VMEM((BLOCKS, 2 * QB, 128), BF16),
            pltpu.VMEM((BLOCKS, 2 * QB, 128), BF16),
            pltpu.VMEM((WINDOW, 128), BF16),
            pltpu.VMEM((WINDOW, 128), BF16),
            pltpu.VMEM((128, WINDOW), BF16),
            pltpu.VMEM((2 * R, WINDOW), BF16),
            pltpu.VMEM((WINDOW, 2 * QB), F32),
            pltpu.VMEM((WINDOW, 2 * QB), F32),
            pltpu.VMEM((WINDOW, 128), F32),
            pltpu.VMEM((WINDOW, 128), F32),
            pltpu.VMEM((2 * R, WINDOW), F32),
            pltpu.VMEM((64, 128), F32),
            pltpu.SMEM((TILES,), jnp.int32),
        ],
        compiler_params=params(56),
        name="attention",
    )(place, info, recv, q_up, v_up, cos_t, sin_t)


def down_kernel(info, back, features, ups, out):
    here = info[0]
    inner = jnp.sum(back[:, 512:544].astype(F32), 0).astype(BF16)
    down = nn(inner, features[...]) * ADAPTER_SCALING
    for d in range(DEVICES):
        g, b = d % 4, d // 4
        up = jnp.where(here == d % TILES, ups[d // TILES], 0.0)
        out[d] = jnp.concatenate(
            [down[g * 8 : g * 8 + 8, b * 128 : b * 128 + 128], up], 0
        ).astype(BF16)


def down(info, back, features, ups):
    return pl.pallas_call(
        down_kernel,
        out_shape=jax.ShapeDtypeStruct((DEVICES, 16, 128), BF16),
        in_specs=[SMEM] + [VMEM] * 3,
        out_specs=VMEM,
        compiler_params=params(24),
        name="down",
    )(info, back, features, ups)


def merge_kernel(parts, out):
    piece = jnp.sum(parts[...].astype(F32), 0).astype(BF16)
    for d in range(DEVICES):
        out[d] = piece


def merge(parts):
    return pl.pallas_call(
        merge_kernel,
        out_shape=jax.ShapeDtypeStruct((DEVICES, 16, 128), BF16),
        in_specs=[VMEM],
        out_specs=VMEM,
        compiler_params=params(16),
        name="merge",
    )(parts)


def unpack_kernel(back, grad_query, grad_key, grad_value):
    for j in range(TILES):
        grad_query[:, j * 256 : j * 256 + 128] = back[j, 0:128]
        grad_query[:, j * 256 + 128 : j * 256 + 256] = back[j, 128:256]
    for h in range(KVH):
        at = slice(h * 128, h * 128 + 128)
        grad_key[:, at] = (
            back[2 * h, 256:384].astype(F32) + back[2 * h + 1, 256:384].astype(F32)
        ).astype(BF16)
        grad_value[:, at] = (
            back[2 * h, 384:512].astype(F32) + back[2 * h + 1, 384:512].astype(F32)
        ).astype(BF16)


def unpack(back):
    return pl.pallas_call(
        unpack_kernel,
        out_shape=(
            jax.ShapeDtypeStruct((TILE, H * DH), BF16),
            jax.ShapeDtypeStruct((TILE, KVH * DH), BF16),
            jax.ShapeDtypeStruct((TILE, KVH * DH), BF16),
        ),
        in_specs=[VMEM],
        out_specs=(VMEM, VMEM, VMEM),
        compiler_params=params(24),
        name="unpack",
    )(back)


def final_kernel(pieces, q_down, q_up, v_down, v_up):
    for b in range(D // 128):
        for g in range(2):
            at = slice(g * 8, g * 8 + 8), slice(b * 128, b * 128 + 128)
            q_down[at] = pieces[4 * b + g].astype(F32)[0:8]
            v_down[at] = pieces[4 * b + 2 + g].astype(F32)[0:8]
    up = [
        [pieces[a * TILES + j].astype(F32)[8:16] for a in range(6)] for j in range(TILES)
    ]
    for j in range(TILES):
        for a in range(4):
            h, r = a // 2, a % 2
            q_up[r * 8 : r * 8 + 8, j * 256 + h * 128 : j * 256 + h * 128 + 128] = up[j][a]
    for h in range(KVH):
        for r in range(2):
            v_up[r * 8 : r * 8 + 8, h * 128 : h * 128 + 128] = (
                up[2 * h][4 + r] + up[2 * h + 1][4 + r]
            )


def final(pieces):
    return pl.pallas_call(
        final_kernel,
        out_shape=(
            jax.ShapeDtypeStruct((R, D), F32),
            jax.ShapeDtypeStruct((R, H * DH), F32),
            jax.ShapeDtypeStruct((R, D), F32),
            jax.ShapeDtypeStruct((R, KVH * DH), F32),
        ),
        in_specs=[VMEM],
        out_specs=(VMEM,) * 4,
        compiler_params=params(24),
        name="final",
    )(pieces)


def exchange(array, axes):
    return lax.all_to_all(array, axes, 0, 0, tiled=True)


def body(
    features,
    queries,
    keys,
    values,
    grad_out,
    lengths,
    placement,
    query_down,
    query_up,
    value_down,
    value_up,
):
    here = lax.axis_index("ctx")
    info = jnp.stack([here.astype(jnp.int32), lengths[0]])
    packed = pack(
        info, features[0], queries[0], keys[0], values[0], grad_out[0], query_down.T, value_down.T
    )
    recv = exchange(packed, "ctx")
    out, ups = attention(placement[0], info, recv, query_up, value_up)
    back = exchange(out, "ctx")
    parts = exchange(down(info, back, features[0], ups), ("dp", "ctx"))
    grad_query, grad_key, grad_value = unpack(back)
    pieces = exchange(merge(parts), ("dp", "ctx"))
    q_down, q_up, v_down, v_up = final(pieces)
    return (grad_query[None], grad_key[None], grad_value[None], q_down.T, q_up, v_down.T, v_up)


def solution(mesh):
    rows = P("dp", "ctx", None)
    return jax.shard_map(
        body,
        mesh=mesh,
        in_specs=(rows,) * 5 + (P("dp"), P("dp", None)) + (P(),) * 4,
        out_specs=(rows,) * 3 + (P(),) * 4,
        check_vma=False,
    )
```

```python
import math

import jax
import jax.numpy as jnp
import numpy as np
from jax import lax
from jax.experimental import pallas as pl
from jax.experimental.pallas import tpu as pltpu
from jax.sharding import PartitionSpec as P

D = 4096
H = 32
KVH = 8
DH = 128
R = 16
TILE = 128
TILES = 16
WINDOW = TILE * TILES
DEVICES = 128
DP = 8
SCALE = 1.0 / math.sqrt(DH)
LOG2E = math.log2(math.e)
ADAPTER_SCALING = 2.0
FAR_BELOW = -1e30
IN_ROWS = 6 * TILE + 2 * R
OUT_ROWS = 4 * TILE + 2 * R
PIECE = 7 * R
PARTS = 4
PACK_COPIES = 3 * PARTS + 6
QB = 256
KB = 256
BLOCKS = WINDOW // QB

F32 = jnp.float32
BF16 = jnp.bfloat16
VMEM = pl.BlockSpec(memory_space=pltpu.VMEM)
SMEM = pl.BlockSpec(memory_space=pltpu.SMEM)
HBM = pl.BlockSpec(memory_space=pltpu.HBM)


def nt(a, b):
    return lax.dot_general(a, b, (((1,), (1,)), ((), ())), preferred_element_type=F32)


def nn(a, b):
    return lax.dot_general(a, b, (((1,), (0,)), ((), ())), preferred_element_type=F32)


def params(mebibytes):
    return pltpu.CompilerParams(vmem_limit_bytes=mebibytes * 1024 * 1024)


def pack_kernel(
    info,
    features,
    queries,
    keys,
    values,
    grad_out,
    q_down,
    v_down,
    out,
    f_in,
    q_in,
    k_in,
    v_in,
    g_in,
    qd_in,
    vd_in,
    held,
    sems,
):
    used = iter(range(PACK_COPIES))

    def copy(source, target):
        made = pltpu.make_async_copy(source, target, sems.at[next(used)])
        made.start()
        return made

    width = D // PARTS
    some = TILES // PARTS
    waits = [copy(keys, k_in), copy(values, v_in)]
    parts = []
    for p in range(PARTS):
        at = slice(p * width, p * width + width)
        parts.append(
            (copy(queries.at[:, at], q_in.at[:, at]), copy(grad_out.at[:, at], g_in.at[:, at]))
        )
    low = [copy(features, f_in), copy(q_down, qd_in), copy(v_down, vd_in)]
    for made in waits:
        made.wait()
    sent = []
    for p in range(PARTS):
        for made in parts[p]:
            made.wait()
        for j in range(p * some, p * some + some):
            h = j // 2
            held[j, 0:128] = q_in[:, j * 256 : j * 256 + 128]
            held[j, 128:256] = q_in[:, j * 256 + 128 : j * 256 + 256]
            held[j, 256:384] = g_in[:, j * 256 : j * 256 + 128]
            held[j, 384:512] = g_in[:, j * 256 + 128 : j * 256 + 256]
            held[j, 512:640] = k_in[:, h * 128 : h * 128 + 128]
            held[j, 640:768] = v_in[:, h * 128 : h * 128 + 128]
        at = pl.ds(p * some, some), pl.ds(0, 6 * TILE)
        sent.append(copy(held.at[at], out.at[at]))
    for made in low:
        made.wait()
    low_q = nt(qd_in[...], f_in[...]).astype(BF16)
    low_v = nt(vd_in[...], f_in[...]).astype(BF16)
    for j in range(TILES):
        held[j, 768:784] = low_q
        held[j, 784:800] = low_v
    at = pl.ds(0, TILES), pl.ds(6 * TILE, 2 * R)
    sent.append(copy(held.at[at], out.at[at]))
    for made in sent:
        made.wait()


def pack(info, features, queries, keys, values, grad_out, q_down, v_down):
    return pl.pallas_call(
        pack_kernel,
        out_shape=jax.ShapeDtypeStruct((TILES, IN_ROWS, 128), BF16),
        in_specs=[SMEM] + [HBM] * 7,
        out_specs=HBM,
        scratch_shapes=[
            pltpu.VMEM((TILE, D), BF16),
            pltpu.VMEM((TILE, D), BF16),
            pltpu.VMEM((TILE, KVH * DH), BF16),
            pltpu.VMEM((TILE, KVH * DH), BF16),
            pltpu.VMEM((TILE, D), BF16),
            pltpu.VMEM((R, D), BF16),
            pltpu.VMEM((R, D), BF16),
            pltpu.VMEM((TILES, IN_ROWS, 128), BF16),
            pltpu.SemaphoreType.DMA((PACK_COPIES,)),
        ],
        compiler_params=params(56),
        name="pack",
    )(info, features, queries, keys, values, grad_out, q_down, v_down)


def rotary(tables, tile, count):
    cos_r, sin_r = tables[0:64], tables[64:128]
    cosine, sine = [], []
    for t in range(tile, tile + count):
        cos_t, sin_t = tables[128:192, t : t + 1], tables[192:256, t : t + 1]
        cosine.append(cos_t * cos_r - sin_t * sin_r)
        sine.append(sin_t * cos_r + cos_t * sin_r)
    return jnp.concatenate(cosine, 1), jnp.concatenate(sine, 1)


def attention_kernel(
    place,
    info,
    recv,
    q_up,
    v_up,
    tables,
    out,
    up_out,
    qs,
    gs,
    ks,
    vs,
    kt,
    low,
    s_all,
    dp_all,
    dk,
    dv,
    inner,
    pre,
    upg,
    inv,
):
    here = info[0]
    length = info[1]
    rows = lax.broadcasted_iota(jnp.int32, (TILE, 128), 0)

    def arrange(t, _):
        p = place[t]
        inv[p] = t
        block = p // 2
        offset = pl.multiple_of((p % 2) * TILE, TILE)
        at = pl.ds(pl.multiple_of(p * TILE, TILE), TILE)
        live = rows + p * TILE < length
        for h in range(2):
            to = pl.ds(pl.multiple_of(h * QB + offset, TILE), TILE)
            qs[block, to] = recv[t, h * 128 : h * 128 + 128]
            grad = recv[t, 256 + h * 128 : 384 + h * 128].astype(F32)
            gs[block, to] = jnp.where(live, grad, 0.0).astype(BF16)
        key = recv[t, 512:640]
        ks[at] = key
        vs[at] = recv[t, 640:768]
        kt[:, at] = key.astype(F32).T.astype(BF16)
        low[:, at] = recv[t, 768:800]
        return 0

    for t in range(TILES):
        arrange(t, 0)
    q_up_here = q_up[:, pl.ds(pl.multiple_of(here * 256, 256), 256)]
    v_up_here = v_up[:, pl.ds(pl.multiple_of((here // 2) * 128, 128), 128)]
    base = SCALE * LOG2E

    def block_step(i, _):
        @pl.when(i * QB < length)
        def _():
            query = qs[i]
            grad = gs[i]

            def first(start, size, carry, diagonal=False):
                peak, total, weighted = carry
                at = pl.ds(start, size)
                s = nt(ks[at], query) * base
                dp = nt(vs[at], grad)
                if diagonal:
                    ki = lax.broadcasted_iota(jnp.int32, (size, 2 * QB), 0) + (start - i * QB)
                    qi = lax.broadcasted_iota(jnp.int32, (size, 2 * QB), 1) & (QB - 1)
                    s = jnp.where(ki <= qi, s, FAR_BELOW)
                s_all[at] = s
                dp_all[at] = dp
                new = jnp.maximum(peak, jnp.max(s, 0, keepdims=True))
                e = jnp.exp2(s - new)
                alpha = jnp.exp2(peak - new)
                total = total * alpha + jnp.sum(e, 0, keepdims=True)
                weighted = weighted * alpha + jnp.sum(e * dp, 0, keepdims=True)
                return new, total, weighted

            zero = jnp.zeros((1, 2 * QB), F32)
            carry = (jnp.full((1, 2 * QB), FAR_BELOW, F32), zero, zero)
            sizes = [(a, min(KB, i * QB - a)) for a in range(0, i * QB, KB)]
            last = [(a, min(KB, QB)) for a in range(i * QB, i * QB + QB, min(KB, QB))]
            for start, size in sizes:
                carry = first(start, size, carry)
            for start, size in last:
                carry = first(start, size, carry, True)
            peak, total, weighted = carry
            lse = peak + jnp.log2(total)
            delta = weighted / total

            def second(start, size, dq):
                at = pl.ds(start, size)
                prob = jnp.exp2(s_all[at] - lse)
                grad_logit = (prob * (dp_all[at] - delta)).astype(BF16)
                if start >= i * QB:
                    dv[at] = nn(prob.astype(BF16), grad)
                    dk[at] = nn(grad_logit, query)
                else:
                    dv[at] += nn(prob.astype(BF16), grad)
                    dk[at] += nn(grad_logit, query)
                return dq + nn(kt[:, at], grad_logit)

            dq = jnp.zeros((128, 2 * QB), F32)
            for start, size in sizes + last:
                dq = second(start, size, dq)
            dq = dq * SCALE
            span = pl.ds(pl.multiple_of(i * QB, QB), QB)
            cosine, sine = rotary(tables, 2 * i, 2)
            for h in range(2):
                a = dq[0:64, h * QB : h * QB + QB]
                b = dq[64:128, h * QB : h * QB + QB]
                pre[h * 128 : h * 128 + 64, span] = (a * cosine + b * sine).astype(BF16)
                pre[h * 128 + 64 : h * 128 + 128, span] = (b * cosine - a * sine).astype(BF16)
                for half in range(2):
                    at = h * QB + half * TILE
                    out[inv[2 * i + half], h * 128 : h * 128 + 128] = dq[
                        :, at : at + TILE
                    ].astype(BF16)

        @pl.when(i * QB >= length)
        def _():
            span = pl.ds(i * QB, QB)
            for half in range(2):
                out[inv[2 * i + half], 0:256] = jnp.zeros((256, 128), BF16)
            dk[span] = jnp.zeros((QB, 128), F32)
            dv[span] = jnp.zeros((QB, 128), F32)
            pre[:, span] = jnp.zeros((256, QB), BF16)

        return 0

    for i in range(BLOCKS):
        block_step(i, 0)

    grad_value = dv[...].astype(BF16)
    inner[0:R] = nn(q_up_here, pre[...]).astype(BF16)
    inner[R : 2 * R] = nt(v_up_here, grad_value).astype(BF16)
    up_q = nt(low[0:R], pre[...])
    upg[0:R] = up_q[:, 0:128]
    upg[R : 2 * R] = up_q[:, 128:256]
    upg[2 * R : 3 * R] = nn(low[R : 2 * R], grad_value)
    for p in range(TILES):
        at = slice(p * TILE, p * TILE + TILE)
        t = inv[p]
        out[t, 256:384] = (dk[at] * SCALE).astype(BF16)
        out[t, 384:512] = dv[at].astype(BF16)
        out[t, 512:544] = inner[:, at]
    up_out[...] = upg[...] * ADAPTER_SCALING


def rotary_tables():
    half = DH // 2
    freq = np.exp(-np.arange(half, dtype=np.float32) * np.float32(math.log(500000.0) / half))
    freq = freq.astype(np.float64)[:, None]
    row = freq * np.arange(TILE)[None, :]
    start = freq * (np.arange(TILE)[None, :] * TILE)
    return np.concatenate([np.cos(row), np.sin(row), np.cos(start), np.sin(start)], 0).astype(
        np.float32
    )


def attention(place, info, recv, q_up, v_up):
    tables = rotary_tables()
    return pl.pallas_call(
        attention_kernel,
        out_shape=(
            jax.ShapeDtypeStruct((TILES, OUT_ROWS, 128), BF16),
            jax.ShapeDtypeStruct((3 * R, 128), F32),
        ),
        in_specs=[SMEM, SMEM] + [VMEM] * 4,
        out_specs=(VMEM, VMEM),
        scratch_shapes=[
            pltpu.VMEM((BLOCKS, 2 * QB, 128), BF16),
            pltpu.VMEM((BLOCKS, 2 * QB, 128), BF16),
            pltpu.VMEM((WINDOW, 128), BF16),
            pltpu.VMEM((WINDOW, 128), BF16),
            pltpu.VMEM((128, WINDOW), BF16),
            pltpu.VMEM((2 * R, WINDOW), BF16),
            pltpu.VMEM((WINDOW, 2 * QB), F32),
            pltpu.VMEM((WINDOW, 2 * QB), F32),
            pltpu.VMEM((WINDOW, 128), F32),
            pltpu.VMEM((WINDOW, 128), F32),
            pltpu.VMEM((2 * R, WINDOW), BF16),
            pltpu.VMEM((2 * DH, WINDOW), BF16),
            pltpu.VMEM((3 * R, 128), F32),
            pltpu.SMEM((TILES,), jnp.int32),
        ],
        compiler_params=params(36),
        name="attention",
    )(place, info, recv, q_up, v_up, tables)


def down_kernel(back, features, out):
    inner = jnp.sum(back[:, 512:544].astype(F32), 0).astype(BF16)
    down = nn(inner, features[...]) * ADAPTER_SCALING
    for j in range(TILES):
        for half in range(2):
            at = j * 256 + half * 128
            out[j, half * 32 : half * 32 + 32] = down[:, at : at + 128].astype(BF16)


def down(back, features):
    return pl.pallas_call(
        down_kernel,
        out_shape=jax.ShapeDtypeStruct((TILES, 4 * R, 128), BF16),
        in_specs=[VMEM] * 2,
        out_specs=VMEM,
        compiler_params=params(24),
        name="down",
    )(back, features)


def chain_kernel(parts, ups, out):
    piece = jnp.sum(parts[...].astype(F32), 0).astype(BF16)
    up = ups[...].astype(BF16)
    for c in range(DP):
        out[c, 0 : 4 * R] = piece
        out[c, 4 * R : PIECE] = up


def chain_sum(parts, ups):
    return pl.pallas_call(
        chain_kernel,
        out_shape=jax.ShapeDtypeStruct((DP, PIECE, 128), BF16),
        in_specs=[VMEM] * 2,
        out_specs=VMEM,
        compiler_params=params(16),
        name="chain_sum",
    )(parts, ups)


def all_kernel(parts, out):
    piece = jnp.sum(parts[...].astype(F32), 0).astype(BF16)
    for j in range(TILES):
        out[j] = piece


def all_sum(parts):
    return pl.pallas_call(
        all_kernel,
        out_shape=jax.ShapeDtypeStruct((TILES, PIECE, 128), BF16),
        in_specs=[VMEM],
        out_specs=VMEM,
        compiler_params=params(16),
        name="all_sum",
    )(parts)


def unpack_kernel(back, grad_query, grad_key, grad_value):
    for j in range(TILES):
        grad_query[:, j * 256 : j * 256 + 128] = back[j, 0:128].astype(F32).T.astype(BF16)
        grad_query[:, j * 256 + 128 : j * 256 + 256] = back[j, 128:256].astype(F32).T.astype(BF16)
    for h in range(KVH):
        at = slice(h * 128, h * 128 + 128)
        grad_key[:, at] = (
            back[2 * h, 256:384].astype(F32) + back[2 * h + 1, 256:384].astype(F32)
        ).astype(BF16)
        grad_value[:, at] = (
            back[2 * h, 384:512].astype(F32) + back[2 * h + 1, 384:512].astype(F32)
        ).astype(BF16)


def unpack(back):
    return pl.pallas_call(
        unpack_kernel,
        out_shape=(
            jax.ShapeDtypeStruct((TILE, H * DH), BF16),
            jax.ShapeDtypeStruct((TILE, KVH * DH), BF16),
            jax.ShapeDtypeStruct((TILE, KVH * DH), BF16),
        ),
        in_specs=[VMEM],
        out_specs=(VMEM, VMEM, VMEM),
        compiler_params=params(24),
        name="unpack",
    )(back)


def final_kernel(pieces, q_down, q_up, v_down, v_up):
    for j in range(TILES):
        piece = pieces[j].astype(F32)
        for half in range(2):
            at = slice(j * 256 + half * 128, j * 256 + half * 128 + 128)
            q_down[:, at] = piece[half * 32 : half * 32 + R]
            v_down[:, at] = piece[half * 32 + R : half * 32 + 2 * R]
            q_up[:, at] = piece[4 * R + half * R : 5 * R + half * R]
    for h in range(KVH):
        v_up[:, h * 128 : h * 128 + 128] = pieces[2 * h, 6 * R : PIECE].astype(F32) + pieces[
            2 * h + 1, 6 * R : PIECE
        ].astype(F32)


def final(pieces):
    return pl.pallas_call(
        final_kernel,
        out_shape=(
            jax.ShapeDtypeStruct((R, D), F32),
            jax.ShapeDtypeStruct((R, H * DH), F32),
            jax.ShapeDtypeStruct((R, D), F32),
            jax.ShapeDtypeStruct((R, KVH * DH), F32),
        ),
        in_specs=[VMEM],
        out_specs=(VMEM,) * 4,
        compiler_params=params(24),
        name="final",
    )(pieces)


def exchange(array, axes):
    return lax.all_to_all(array, axes, 0, 0, tiled=True)


def body(
    features,
    queries,
    keys,
    values,
    grad_out,
    lengths,
    placement,
    query_down,
    query_up,
    value_down,
    value_up,
):
    here = lax.axis_index("ctx")
    info = jnp.stack([here.astype(jnp.int32), lengths[0]])
    packed = pack(
        info, features[0], queries[0], keys[0], values[0], grad_out[0], query_down.T, value_down.T
    )
    recv = exchange(packed, "ctx")
    out, ups = attention(placement[0], info, recv, query_up, value_up)
    back = exchange(out, "ctx")
    parts = exchange(down(back, features[0]), "ctx")
    parts = exchange(chain_sum(parts, ups), "dp")
    grad_query, grad_key, grad_value = unpack(back)
    pieces = exchange(all_sum(parts), "ctx")
    q_down, q_up, v_down, v_up = final(pieces)
    return (grad_query[None], grad_key[None], grad_value[None], q_down.T, q_up, v_down.T, v_up)


def solution(mesh):
    rows = P("dp", "ctx", None)
    return jax.shard_map(
        body,
        mesh=mesh,
        in_specs=(rows,) * 5 + (P("dp"), P("dp", None)) + (P(),) * 4,
        out_specs=(rows,) * 3 + (P(),) * 4,
        check_vma=False,
    )
```

```python
import math

import jax
import jax.numpy as jnp
import numpy as np
from jax import lax
from jax.experimental import pallas as pl
from jax.experimental.pallas import tpu as pltpu
from jax.sharding import PartitionSpec as P

D = 4096
H = 32
KVH = 8
DH = 128
R = 16
TILE = 128
TILES = 16
WINDOW = TILE * TILES
DEVICES = 128
DP = 8
SCALE = 1.0 / math.sqrt(DH)
LOG2E = math.log2(math.e)
ADAPTER_SCALING = 2.0
FAR_BELOW = -1e30
IN_ROWS = 6 * TILE + 2 * R
OUT_ROWS = 4 * TILE + 2 * R
PIECE = 7 * R
PARTS = 4
PACK_COPIES = 3 * PARTS + 6
QB = 256
KB = 256
BLOCKS = WINDOW // QB

F32 = jnp.float32
BF16 = jnp.bfloat16
VMEM = pl.BlockSpec(memory_space=pltpu.VMEM)
SMEM = pl.BlockSpec(memory_space=pltpu.SMEM)
HBM = pl.BlockSpec(memory_space=pltpu.HBM)


def nt(a, b):
    return lax.dot_general(a, b, (((1,), (1,)), ((), ())), preferred_element_type=F32)


def nn(a, b):
    return lax.dot_general(a, b, (((1,), (0,)), ((), ())), preferred_element_type=F32)


def params(mebibytes):
    return pltpu.CompilerParams(vmem_limit_bytes=mebibytes * 1024 * 1024)


def pack_kernel(
    place,
    lengths,
    features,
    queries,
    keys,
    values,
    grad_out,
    q_down,
    v_down,
    out,
    f_in,
    q_in,
    k_in,
    v_in,
    g_in,
    qd_in,
    vd_in,
    held,
    sems,
):
    used = iter(range(PACK_COPIES))

    def copy(source, target):
        made = pltpu.make_async_copy(source, target, sems.at[next(used)])
        made.start()
        return made

    width = D // PARTS
    some = TILES // PARTS
    waits = [copy(keys, k_in), copy(values, v_in)]
    parts = []
    for p in range(PARTS):
        at = slice(p * width, p * width + width)
        parts.append(
            (copy(queries.at[:, at], q_in.at[:, at]), copy(grad_out.at[:, at], g_in.at[:, at]))
        )
    low = [copy(features, f_in), copy(q_down, qd_in), copy(v_down, vd_in)]
    for made in waits:
        made.wait()
    sent = []
    for p in range(PARTS):
        for made in parts[p]:
            made.wait()
        for j in range(p * some, p * some + some):
            h = j // 2
            held[j, 0:128] = q_in[:, j * 256 : j * 256 + 128]
            held[j, 128:256] = q_in[:, j * 256 + 128 : j * 256 + 256]
            held[j, 256:384] = g_in[:, j * 256 : j * 256 + 128]
            held[j, 384:512] = g_in[:, j * 256 + 128 : j * 256 + 256]
            held[j, 512:640] = k_in[:, h * 128 : h * 128 + 128]
            held[j, 640:768] = v_in[:, h * 128 : h * 128 + 128]
        at = pl.ds(p * some, some), pl.ds(0, 6 * TILE)
        sent.append(copy(held.at[at], out.at[at]))
    for made in low:
        made.wait()
    low_q = nt(qd_in[...], f_in[...]).astype(BF16)
    low_v = nt(vd_in[...], f_in[...]).astype(BF16)
    for j in range(TILES):
        held[j, 768:784] = low_q
        held[j, 784:800] = low_v
    at = pl.ds(0, TILES), pl.ds(6 * TILE, 2 * R)
    sent.append(copy(held.at[at], out.at[at]))
    for made in sent:
        made.wait()


def pack(place, lengths, features, queries, keys, values, grad_out, q_down, v_down):
    return pl.pallas_call(
        pack_kernel,
        out_shape=jax.ShapeDtypeStruct((TILES, IN_ROWS, 128), BF16),
        in_specs=[SMEM] * 2 + [HBM] * 7,
        out_specs=HBM,
        scratch_shapes=[
            pltpu.VMEM((TILE, D), BF16),
            pltpu.VMEM((TILE, D), BF16),
            pltpu.VMEM((TILE, KVH * DH), BF16),
            pltpu.VMEM((TILE, KVH * DH), BF16),
            pltpu.VMEM((TILE, D), BF16),
            pltpu.VMEM((R, D), BF16),
            pltpu.VMEM((R, D), BF16),
            pltpu.VMEM((TILES, IN_ROWS, 128), BF16),
            pltpu.SemaphoreType.DMA((PACK_COPIES,)),
        ],
        compiler_params=params(56),
        name="pack",
    )(place, lengths, features, queries, keys, values, grad_out, q_down, v_down)


def rotary(tables, tile, count):
    cos_r, sin_r = tables[0:64], tables[64:128]
    cosine, sine = [], []
    for t in range(tile, tile + count):
        cos_t, sin_t = tables[128:192, t : t + 1], tables[192:256, t : t + 1]
        cosine.append(cos_t * cos_r - sin_t * sin_r)
        sine.append(sin_t * cos_r + cos_t * sin_r)
    return jnp.concatenate(cosine, 1), jnp.concatenate(sine, 1)


def attention_kernel(
    place,
    lengths,
    recv,
    q_up,
    v_up,
    tables,
    out,
    up_out,
    qs,
    gs,
    ks,
    vs,
    kt,
    low,
    s_all,
    dp_all,
    dk,
    dv,
    inner,
    pre,
    upg,
    inv,
):
    here = lax.axis_index("ctx")
    length = lengths[0]
    rows = lax.broadcasted_iota(jnp.int32, (TILE, 128), 0)

    def arrange(t, _):
        p = place[t]
        inv[p] = t
        block = p // 2
        offset = pl.multiple_of((p % 2) * TILE, TILE)
        at = pl.ds(pl.multiple_of(p * TILE, TILE), TILE)
        live = rows + p * TILE < length
        for h in range(2):
            to = pl.ds(pl.multiple_of(h * QB + offset, TILE), TILE)
            qs[block, to] = recv[t, h * 128 : h * 128 + 128]
            grad = recv[t, 256 + h * 128 : 384 + h * 128].astype(F32)
            gs[block, to] = jnp.where(live, grad, 0.0).astype(BF16)
        key = recv[t, 512:640]
        ks[at] = key
        vs[at] = recv[t, 640:768]
        low[:, at] = recv[t, 768:800]
        return 0

    for t in range(TILES):
        arrange(t, 0)
    one = lax.broadcasted_iota(jnp.int32, (128, 128), 0) == lax.broadcasted_iota(
        jnp.int32, (128, 128), 1
    )
    kt[...] = nt(jnp.where(one, 1.0, 0.0).astype(BF16), ks[...]).astype(BF16)
    q_up_here = q_up[:, pl.ds(pl.multiple_of(here * 256, 256), 256)]
    v_up_here = v_up[:, pl.ds(pl.multiple_of((here // 2) * 128, 128), 128)]
    base = SCALE * LOG2E

    def block_step(i, _):
        @pl.when(i * QB < length)
        def _():
            query = qs[i]
            grad = gs[i]

            def first(start, size, carry, diagonal=False):
                peak, total, weighted = carry
                at = pl.ds(start, size)
                s = nt(ks[at], query) * base
                dp = nt(vs[at], grad)
                if diagonal:
                    ki = lax.broadcasted_iota(jnp.int32, (size, 2 * QB), 0) + (start - i * QB)
                    qi = lax.broadcasted_iota(jnp.int32, (size, 2 * QB), 1) & (QB - 1)
                    s = jnp.where(ki <= qi, s, FAR_BELOW)
                s_all[at] = s
                dp_all[at] = dp
                new = jnp.maximum(peak, jnp.max(s, 0, keepdims=True))
                e = jnp.exp2(s - new)
                alpha = jnp.exp2(peak - new)
                total = total * alpha + jnp.sum(e, 0, keepdims=True)
                weighted = weighted * alpha + jnp.sum(e * dp, 0, keepdims=True)
                return new, total, weighted

            zero = jnp.zeros((1, 2 * QB), F32)
            carry = (jnp.full((1, 2 * QB), FAR_BELOW, F32), zero, zero)
            sizes = [(a, min(KB, i * QB - a)) for a in range(0, i * QB, KB)]
            last = [(a, min(KB, QB)) for a in range(i * QB, i * QB + QB, min(KB, QB))]
            for start, size in sizes:
                carry = first(start, size, carry)
            for start, size in last:
                carry = first(start, size, carry, True)
            peak, total, weighted = carry
            lse = peak + jnp.log2(total)
            delta = weighted / total

            def second(start, size, dq):
                at = pl.ds(start, size)
                prob = jnp.exp2(s_all[at] - lse)
                grad_logit = (prob * (dp_all[at] - delta)).astype(BF16)
                if start >= i * QB:
                    dv[at] = nn(prob.astype(BF16), grad)
                    dk[at] = nn(grad_logit, query)
                else:
                    dv[at] += nn(prob.astype(BF16), grad)
                    dk[at] += nn(grad_logit, query)
                return dq + nn(kt[:, at], grad_logit)

            dq = jnp.zeros((128, 2 * QB), F32)
            for start, size in sizes + last:
                dq = second(start, size, dq)
            dq = dq * SCALE
            span = pl.ds(pl.multiple_of(i * QB, QB), QB)
            cosine, sine = rotary(tables, 2 * i, 2)
            for h in range(2):
                a = dq[0:64, h * QB : h * QB + QB]
                b = dq[64:128, h * QB : h * QB + QB]
                pre[h * 128 : h * 128 + 64, span] = (a * cosine + b * sine).astype(BF16)
                pre[h * 128 + 64 : h * 128 + 128, span] = (b * cosine - a * sine).astype(BF16)
                for half in range(2):
                    at = h * QB + half * TILE
                    out[inv[2 * i + half], h * 128 : h * 128 + 128] = dq[
                        :, at : at + TILE
                    ].astype(BF16)

        @pl.when(i * QB >= length)
        def _():
            span = pl.ds(i * QB, QB)
            for half in range(2):
                out[inv[2 * i + half], 0:256] = jnp.zeros((256, 128), BF16)
            dk[span] = jnp.zeros((QB, 128), F32)
            dv[span] = jnp.zeros((QB, 128), F32)
            pre[:, span] = jnp.zeros((256, QB), BF16)

        return 0

    for i in range(BLOCKS):
        block_step(i, 0)

    grad_value = dv[...].astype(BF16)
    inner[0:R] = nn(q_up_here, pre[...]).astype(BF16)
    inner[R : 2 * R] = nt(v_up_here, grad_value).astype(BF16)
    up_q = nt(low[0:R], pre[...])
    upg[0:R] = up_q[:, 0:128]
    upg[R : 2 * R] = up_q[:, 128:256]
    upg[2 * R : 3 * R] = nn(low[R : 2 * R], grad_value)
    for p in range(TILES):
        at = slice(p * TILE, p * TILE + TILE)
        t = inv[p]
        out[t, 256:384] = (dk[at] * SCALE).astype(BF16)
        out[t, 384:512] = dv[at].astype(BF16)
        out[t, 512:544] = inner[:, at]
    up_out[...] = upg[...] * ADAPTER_SCALING


def rotary_tables():
    half = DH // 2
    freq = np.exp(-np.arange(half, dtype=np.float32) * np.float32(math.log(500000.0) / half))
    freq = freq.astype(np.float64)[:, None]
    row = freq * np.arange(TILE)[None, :]
    start = freq * (np.arange(TILE)[None, :] * TILE)
    return np.concatenate([np.cos(row), np.sin(row), np.cos(start), np.sin(start)], 0).astype(
        np.float32
    )


def attention(place, lengths, recv, q_up, v_up):
    tables = rotary_tables()
    return pl.pallas_call(
        attention_kernel,
        out_shape=(
            jax.ShapeDtypeStruct((TILES, OUT_ROWS, 128), BF16),
            jax.ShapeDtypeStruct((3 * R, 128), F32),
        ),
        in_specs=[SMEM, SMEM] + [VMEM] * 4,
        out_specs=(VMEM, VMEM),
        scratch_shapes=[
            pltpu.VMEM((BLOCKS, 2 * QB, 128), BF16),
            pltpu.VMEM((BLOCKS, 2 * QB, 128), BF16),
            pltpu.VMEM((WINDOW, 128), BF16),
            pltpu.VMEM((WINDOW, 128), BF16),
            pltpu.VMEM((128, WINDOW), BF16),
            pltpu.VMEM((2 * R, WINDOW), BF16),
            pltpu.VMEM((WINDOW, 2 * QB), F32),
            pltpu.VMEM((WINDOW, 2 * QB), F32),
            pltpu.VMEM((WINDOW, 128), F32),
            pltpu.VMEM((WINDOW, 128), F32),
            pltpu.VMEM((2 * R, WINDOW), BF16),
            pltpu.VMEM((2 * DH, WINDOW), BF16),
            pltpu.VMEM((3 * R, 128), F32),
            pltpu.SMEM((TILES,), jnp.int32),
        ],
        compiler_params=params(36),
        name="attention",
    )(place, lengths, recv, q_up, v_up, tables)


def down_kernel(back, features, out):
    inner = jnp.sum(back[:, 512:544].astype(F32), 0).astype(BF16)
    down = nn(inner, features[...]) * ADAPTER_SCALING
    for j in range(TILES):
        for half in range(2):
            at = j * 256 + half * 128
            out[j, half * 32 : half * 32 + 32] = down[:, at : at + 128].astype(BF16)


def down(back, features):
    return pl.pallas_call(
        down_kernel,
        out_shape=jax.ShapeDtypeStruct((TILES, 4 * R, 128), BF16),
        in_specs=[VMEM] * 2,
        out_specs=VMEM,
        compiler_params=params(24),
        name="down",
    )(back, features)


def chain_kernel(parts, ups, out):
    piece = jnp.sum(parts[...].astype(F32), 0).astype(BF16)
    up = ups[...].astype(BF16)
    for c in range(DP):
        out[c, 0 : 4 * R] = piece
        out[c, 4 * R : PIECE] = up


def chain_sum(parts, ups):
    return pl.pallas_call(
        chain_kernel,
        out_shape=jax.ShapeDtypeStruct((DP, PIECE, 128), BF16),
        in_specs=[VMEM] * 2,
        out_specs=VMEM,
        compiler_params=params(16),
        name="chain_sum",
    )(parts, ups)


def all_kernel(parts, out):
    piece = jnp.sum(parts[...].astype(F32), 0).astype(BF16)
    for j in range(TILES):
        out[j] = piece


def all_sum(parts):
    return pl.pallas_call(
        all_kernel,
        out_shape=jax.ShapeDtypeStruct((TILES, PIECE, 128), BF16),
        in_specs=[VMEM],
        out_specs=VMEM,
        compiler_params=params(16),
        name="all_sum",
    )(parts)


def unpack_kernel(back, grad_query, grad_key, grad_value):
    for j in range(TILES):
        grad_query[:, j * 256 : j * 256 + 128] = back[j, 0:128].astype(F32).T.astype(BF16)
        grad_query[:, j * 256 + 128 : j * 256 + 256] = back[j, 128:256].astype(F32).T.astype(BF16)
    for h in range(KVH):
        at = slice(h * 128, h * 128 + 128)
        grad_key[:, at] = (
            back[2 * h, 256:384].astype(F32) + back[2 * h + 1, 256:384].astype(F32)
        ).astype(BF16)
        grad_value[:, at] = (
            back[2 * h, 384:512].astype(F32) + back[2 * h + 1, 384:512].astype(F32)
        ).astype(BF16)


def unpack(back):
    return pl.pallas_call(
        unpack_kernel,
        out_shape=(
            jax.ShapeDtypeStruct((TILE, H * DH), BF16),
            jax.ShapeDtypeStruct((TILE, KVH * DH), BF16),
            jax.ShapeDtypeStruct((TILE, KVH * DH), BF16),
        ),
        in_specs=[VMEM],
        out_specs=(VMEM, VMEM, VMEM),
        compiler_params=params(24),
        name="unpack",
    )(back)


def final_kernel(pieces, q_down, q_up, v_down, v_up):
    for j in range(TILES):
        piece = pieces[j].astype(F32)
        for half in range(2):
            at = slice(j * 256 + half * 128, j * 256 + half * 128 + 128)
            q_down[:, at] = piece[half * 32 : half * 32 + R]
            v_down[:, at] = piece[half * 32 + R : half * 32 + 2 * R]
            q_up[:, at] = piece[4 * R + half * R : 5 * R + half * R]
    for h in range(KVH):
        v_up[:, h * 128 : h * 128 + 128] = pieces[2 * h, 6 * R : PIECE].astype(F32) + pieces[
            2 * h + 1, 6 * R : PIECE
        ].astype(F32)


def final(pieces):
    return pl.pallas_call(
        final_kernel,
        out_shape=(
            jax.ShapeDtypeStruct((R, D), F32),
            jax.ShapeDtypeStruct((R, H * DH), F32),
            jax.ShapeDtypeStruct((R, D), F32),
            jax.ShapeDtypeStruct((R, KVH * DH), F32),
        ),
        in_specs=[VMEM],
        out_specs=(VMEM,) * 4,
        compiler_params=params(24),
        name="final",
    )(pieces)


def exchange(array, axes):
    return lax.all_to_all(array, axes, 0, 0, tiled=True)


def body(
    features,
    queries,
    keys,
    values,
    grad_out,
    lengths,
    placement,
    query_down,
    query_up,
    value_down,
    value_up,
):
    packed = pack(
        placement[0], lengths, features[0], queries[0], keys[0], values[0], grad_out[0], query_down.T, value_down.T
    )
    recv = exchange(packed, "ctx")
    out, ups = attention(placement[0], lengths, recv, query_up, value_up)
    back = exchange(out, "ctx")
    parts = exchange(down(back, features[0]), "ctx")
    parts = exchange(chain_sum(parts, ups), "dp")
    grad_query, grad_key, grad_value = unpack(back)
    pieces = exchange(all_sum(parts), "ctx")
    q_down, q_up, v_down, v_up = final(pieces)
    return (grad_query[None], grad_key[None], grad_value[None], q_down.T, q_up, v_down.T, v_up)


def solution(mesh):
    rows = P("dp", "ctx", None)
    return jax.shard_map(
        body,
        mesh=mesh,
        in_specs=(rows,) * 5 + (P("dp"), P("dp", None)) + (P(),) * 4,
        out_specs=(rows,) * 3 + (P(),) * 4,
        check_vma=False,
    )
```

```python
import math

import jax
import jax.numpy as jnp
import numpy as np
from jax import lax
from jax.experimental import pallas as pl
from jax.experimental.pallas import tpu as pltpu
from jax.sharding import PartitionSpec as P

D = 4096
H = 32
KVH = 8
DH = 128
R = 16
TILE = 128
TILES = 16
WINDOW = TILE * TILES
DEVICES = 128
DP = 8
SCALE = 1.0 / math.sqrt(DH)
LOG2E = math.log2(math.e)
ADAPTER_SCALING = 2.0
FAR_BELOW = -1e30
IN_ROWS = 6 * TILE + 2 * R
OUT_ROWS = 4 * TILE + 2 * R
PIECE = 7 * R
PARTS = 4
PACK_COPIES = 3 * PARTS + 5
QB = 256
KB = 256
BLOCKS = WINDOW // QB

F32 = jnp.float32
BF16 = jnp.bfloat16
VMEM = pl.BlockSpec(memory_space=pltpu.VMEM)
SMEM = pl.BlockSpec(memory_space=pltpu.SMEM)
HBM = pl.BlockSpec(memory_space=pltpu.HBM)


def nt(a, b):
    return lax.dot_general(a, b, (((1,), (1,)), ((), ())), preferred_element_type=F32)


def nn(a, b):
    return lax.dot_general(a, b, (((1,), (0,)), ((), ())), preferred_element_type=F32)


def params(mebibytes):
    return pltpu.CompilerParams(vmem_limit_bytes=mebibytes * 1024 * 1024)


def pack_kernel(
    place,
    lengths,
    features,
    queries,
    keys,
    values,
    grad_out,
    q_down,
    v_down,
    out,
    f_in,
    q_in,
    k_in,
    v_in,
    g_in,
    qd_in,
    vd_in,
    held,
    sems,
):
    used = iter(range(PACK_COPIES))

    def copy(source, target):
        made = pltpu.make_async_copy(source, target, sems.at[next(used)])
        made.start()
        return made

    width = D // PARTS
    some = TILES // PARTS
    low = [copy(features, f_in), copy(q_down, qd_in), copy(v_down, vd_in)]
    waits = [copy(keys, k_in), copy(values, v_in)]
    parts = []
    for p in range(PARTS):
        at = slice(p * width, p * width + width)
        parts.append(
            (copy(queries.at[:, at], q_in.at[:, at]), copy(grad_out.at[:, at], g_in.at[:, at]))
        )
    for made in low:
        made.wait()
    low_q = nt(qd_in[...], f_in[...]).astype(BF16)
    low_v = nt(vd_in[...], f_in[...]).astype(BF16)
    for j in range(TILES):
        held[j, 768:784] = low_q
        held[j, 784:800] = low_v
    for made in waits:
        made.wait()
    sent = []
    for p in range(PARTS):
        for made in parts[p]:
            made.wait()
        for j in range(p * some, p * some + some):
            h = j // 2
            held[j, 0:128] = q_in[:, j * 256 : j * 256 + 128]
            held[j, 128:256] = q_in[:, j * 256 + 128 : j * 256 + 256]
            held[j, 256:384] = g_in[:, j * 256 : j * 256 + 128]
            held[j, 384:512] = g_in[:, j * 256 + 128 : j * 256 + 256]
            held[j, 512:640] = k_in[:, h * 128 : h * 128 + 128]
            held[j, 640:768] = v_in[:, h * 128 : h * 128 + 128]
        at = pl.ds(p * some, some)
        sent.append(copy(held.at[at], out.at[at]))
    for made in sent:
        made.wait()


def pack(place, lengths, features, queries, keys, values, grad_out, q_down, v_down):
    return pl.pallas_call(
        pack_kernel,
        out_shape=jax.ShapeDtypeStruct((TILES, IN_ROWS, 128), BF16),
        in_specs=[SMEM] * 2 + [HBM] * 7,
        out_specs=HBM,
        scratch_shapes=[
            pltpu.VMEM((TILE, D), BF16),
            pltpu.VMEM((TILE, D), BF16),
            pltpu.VMEM((TILE, KVH * DH), BF16),
            pltpu.VMEM((TILE, KVH * DH), BF16),
            pltpu.VMEM((TILE, D), BF16),
            pltpu.VMEM((R, D), BF16),
            pltpu.VMEM((R, D), BF16),
            pltpu.VMEM((TILES, IN_ROWS, 128), BF16),
            pltpu.SemaphoreType.DMA((PACK_COPIES,)),
        ],
        compiler_params=params(56),
        name="pack",
    )(place, lengths, features, queries, keys, values, grad_out, q_down, v_down)


def rotary(tables, tile, count):
    cos_r, sin_r = tables[0:64], tables[64:128]
    cosine, sine = [], []
    for t in range(tile, tile + count):
        cos_t, sin_t = tables[128:192, t : t + 1], tables[192:256, t : t + 1]
        cosine.append(cos_t * cos_r - sin_t * sin_r)
        sine.append(sin_t * cos_r + cos_t * sin_r)
    return jnp.concatenate(cosine, 1), jnp.concatenate(sine, 1)


def attention_kernel(
    place,
    lengths,
    recv,
    q_up,
    v_up,
    tables,
    out,
    up_out,
    qs,
    gs,
    ks,
    vs,
    kt,
    low,
    s_all,
    dp_all,
    dk,
    dv,
    inner,
    pre,
    upg,
    inv,
):
    here = lax.axis_index("ctx")
    length = lengths[0]
    rows = lax.broadcasted_iota(jnp.int32, (TILE, 128), 0)

    def arrange(t, _):
        p = place[t]
        inv[p] = t
        block = p // 2
        offset = pl.multiple_of((p % 2) * TILE, TILE)
        at = pl.ds(pl.multiple_of(p * TILE, TILE), TILE)
        live = rows + p * TILE < length
        for h in range(2):
            to = pl.ds(pl.multiple_of(h * QB + offset, TILE), TILE)
            qs[block, to] = recv[t, h * 128 : h * 128 + 128]
            grad = recv[t, 256 + h * 128 : 384 + h * 128].astype(F32)
            gs[block, to] = jnp.where(live, grad, 0.0).astype(BF16)
        key = recv[t, 512:640]
        ks[at] = key
        vs[at] = recv[t, 640:768]
        low[:, at] = recv[t, 768:800]
        return 0

    for t in range(TILES):
        arrange(t, 0)
    one = lax.broadcasted_iota(jnp.int32, (128, 128), 0) == lax.broadcasted_iota(
        jnp.int32, (128, 128), 1
    )
    kt[...] = nt(jnp.where(one, 1.0, 0.0).astype(BF16), ks[...]).astype(BF16)
    q_up_here = q_up[:, pl.ds(pl.multiple_of(here * 256, 256), 256)]
    v_up_here = v_up[:, pl.ds(pl.multiple_of((here // 2) * 128, 128), 128)]
    base = SCALE * LOG2E

    def block_step(i, _):
        @pl.when(i * QB < length)
        def _():
            query = qs[i]
            grad = gs[i]

            def first(start, size, carry, diagonal=False):
                peak, total, weighted = carry
                at = pl.ds(start, size)
                s = nt(ks[at], query) * base
                dp = nt(vs[at], grad)
                if diagonal:
                    ki = lax.broadcasted_iota(jnp.int32, (size, 2 * QB), 0) + (start - i * QB)
                    qi = lax.broadcasted_iota(jnp.int32, (size, 2 * QB), 1) & (QB - 1)
                    s = jnp.where(ki <= qi, s, FAR_BELOW)
                s_all[at] = s
                dp_all[at] = dp
                new = jnp.maximum(peak, jnp.max(s, 0, keepdims=True))
                e = jnp.exp2(s - new)
                alpha = jnp.exp2(peak - new)
                total = total * alpha + jnp.sum(e, 0, keepdims=True)
                weighted = weighted * alpha + jnp.sum(e * dp, 0, keepdims=True)
                return new, total, weighted

            zero = jnp.zeros((1, 2 * QB), F32)
            carry = (jnp.full((1, 2 * QB), FAR_BELOW, F32), zero, zero)
            sizes = [(a, min(KB, i * QB - a)) for a in range(0, i * QB, KB)]
            last = [(a, min(KB, QB)) for a in range(i * QB, i * QB + QB, min(KB, QB))]
            for start, size in sizes:
                carry = first(start, size, carry)
            for start, size in last:
                carry = first(start, size, carry, True)
            peak, total, weighted = carry
            lse = peak + jnp.log2(total)
            delta = weighted / total

            def second(start, size, dq):
                at = pl.ds(start, size)
                prob = jnp.exp2(s_all[at] - lse)
                grad_logit = (prob * (dp_all[at] - delta)).astype(BF16)
                if start >= i * QB:
                    dv[at] = nn(prob.astype(BF16), grad)
                    dk[at] = nn(grad_logit, query)
                else:
                    dv[at] += nn(prob.astype(BF16), grad)
                    dk[at] += nn(grad_logit, query)
                return dq + nn(kt[:, at], grad_logit)

            dq = jnp.zeros((128, 2 * QB), F32)
            for start, size in sizes + last:
                dq = second(start, size, dq)
            dq = dq * SCALE
            span = pl.ds(pl.multiple_of(i * QB, QB), QB)
            cosine, sine = rotary(tables, 2 * i, 2)
            for h in range(2):
                a = dq[0:64, h * QB : h * QB + QB]
                b = dq[64:128, h * QB : h * QB + QB]
                pre[h * 128 : h * 128 + 64, span] = (a * cosine + b * sine).astype(BF16)
                pre[h * 128 + 64 : h * 128 + 128, span] = (b * cosine - a * sine).astype(BF16)
                for half in range(2):
                    at = h * QB + half * TILE
                    out[inv[2 * i + half], h * 128 : h * 128 + 128] = dq[
                        :, at : at + TILE
                    ].astype(BF16)

        @pl.when(i * QB >= length)
        def _():
            span = pl.ds(i * QB, QB)
            for half in range(2):
                out[inv[2 * i + half], 0:256] = jnp.zeros((256, 128), BF16)
            dk[span] = jnp.zeros((QB, 128), F32)
            dv[span] = jnp.zeros((QB, 128), F32)
            pre[:, span] = jnp.zeros((256, QB), BF16)

        return 0

    for i in range(BLOCKS):
        block_step(i, 0)

    grad_value = dv[...].astype(BF16)
    inner[0:R] = nn(q_up_here, pre[...]).astype(BF16)
    inner[R : 2 * R] = nt(v_up_here, grad_value).astype(BF16)
    up_q = nt(low[0:R], pre[...])
    upg[0:R] = up_q[:, 0:128]
    upg[R : 2 * R] = up_q[:, 128:256]
    upg[2 * R : 3 * R] = nn(low[R : 2 * R], grad_value)
    for p in range(TILES):
        at = slice(p * TILE, p * TILE + TILE)
        t = inv[p]
        out[t, 256:384] = (dk[at] * SCALE).astype(BF16)
        out[t, 384:512] = dv[at].astype(BF16)
        out[t, 512:544] = inner[:, at]
    up_out[...] = upg[...] * ADAPTER_SCALING


def rotary_tables():
    half = DH // 2
    freq = np.exp(-np.arange(half, dtype=np.float32) * np.float32(math.log(500000.0) / half))
    freq = freq.astype(np.float64)[:, None]
    row = freq * np.arange(TILE)[None, :]
    start = freq * (np.arange(TILE)[None, :] * TILE)
    return np.concatenate([np.cos(row), np.sin(row), np.cos(start), np.sin(start)], 0).astype(
        np.float32
    )


def attention(place, lengths, recv, q_up, v_up):
    tables = rotary_tables()
    return pl.pallas_call(
        attention_kernel,
        out_shape=(
            jax.ShapeDtypeStruct((TILES, OUT_ROWS, 128), BF16),
            jax.ShapeDtypeStruct((3 * R, 128), F32),
        ),
        in_specs=[SMEM, SMEM] + [VMEM] * 4,
        out_specs=(VMEM, VMEM),
        scratch_shapes=[
            pltpu.VMEM((BLOCKS, 2 * QB, 128), BF16),
            pltpu.VMEM((BLOCKS, 2 * QB, 128), BF16),
            pltpu.VMEM((WINDOW, 128), BF16),
            pltpu.VMEM((WINDOW, 128), BF16),
            pltpu.VMEM((128, WINDOW), BF16),
            pltpu.VMEM((2 * R, WINDOW), BF16),
            pltpu.VMEM((WINDOW, 2 * QB), F32),
            pltpu.VMEM((WINDOW, 2 * QB), F32),
            pltpu.VMEM((WINDOW, 128), F32),
            pltpu.VMEM((WINDOW, 128), F32),
            pltpu.VMEM((2 * R, WINDOW), BF16),
            pltpu.VMEM((2 * DH, WINDOW), BF16),
            pltpu.VMEM((3 * R, 128), F32),
            pltpu.SMEM((TILES,), jnp.int32),
        ],
        compiler_params=params(36),
        name="attention",
    )(place, lengths, recv, q_up, v_up, tables)


def down_kernel(back, features, out):
    inner = jnp.sum(back[:, 512:544].astype(F32), 0).astype(BF16)
    down = nn(inner, features[...]) * ADAPTER_SCALING
    for j in range(TILES):
        for half in range(2):
            at = j * 256 + half * 128
            out[j, half * 32 : half * 32 + 32] = down[:, at : at + 128].astype(BF16)


def down(back, features):
    return pl.pallas_call(
        down_kernel,
        out_shape=jax.ShapeDtypeStruct((TILES, 4 * R, 128), BF16),
        in_specs=[VMEM] * 2,
        out_specs=VMEM,
        compiler_params=params(24),
        name="down",
    )(back, features)


def chain_kernel(parts, ups, out):
    piece = jnp.sum(parts[...].astype(F32), 0).astype(BF16)
    up = ups[...].astype(BF16)
    for c in range(DP):
        out[c, 0 : 4 * R] = piece
        out[c, 4 * R : PIECE] = up


def chain_sum(parts, ups):
    return pl.pallas_call(
        chain_kernel,
        out_shape=jax.ShapeDtypeStruct((DP, PIECE, 128), BF16),
        in_specs=[VMEM] * 2,
        out_specs=VMEM,
        compiler_params=params(16),
        name="chain_sum",
    )(parts, ups)


def all_kernel(parts, out):
    piece = jnp.sum(parts[...].astype(F32), 0).astype(BF16)
    for j in range(TILES):
        out[j] = piece


def all_sum(parts):
    return pl.pallas_call(
        all_kernel,
        out_shape=jax.ShapeDtypeStruct((TILES, PIECE, 128), BF16),
        in_specs=[VMEM],
        out_specs=VMEM,
        compiler_params=params(16),
        name="all_sum",
    )(parts)


def unpack_kernel(back, grad_query, grad_key, grad_value):
    for j in range(TILES):
        grad_query[:, j * 256 : j * 256 + 128] = back[j, 0:128].astype(F32).T.astype(BF16)
        grad_query[:, j * 256 + 128 : j * 256 + 256] = back[j, 128:256].astype(F32).T.astype(BF16)
    for h in range(KVH):
        at = slice(h * 128, h * 128 + 128)
        grad_key[:, at] = (
            back[2 * h, 256:384].astype(F32) + back[2 * h + 1, 256:384].astype(F32)
        ).astype(BF16)
        grad_value[:, at] = (
            back[2 * h, 384:512].astype(F32) + back[2 * h + 1, 384:512].astype(F32)
        ).astype(BF16)


def unpack(back):
    return pl.pallas_call(
        unpack_kernel,
        out_shape=(
            jax.ShapeDtypeStruct((TILE, H * DH), BF16),
            jax.ShapeDtypeStruct((TILE, KVH * DH), BF16),
            jax.ShapeDtypeStruct((TILE, KVH * DH), BF16),
        ),
        in_specs=[VMEM],
        out_specs=(VMEM, VMEM, VMEM),
        compiler_params=params(24),
        name="unpack",
    )(back)


def final_kernel(pieces, q_down, q_up, v_down, v_up):
    for j in range(TILES):
        piece = pieces[j].astype(F32)
        for half in range(2):
            at = slice(j * 256 + half * 128, j * 256 + half * 128 + 128)
            q_down[:, at] = piece[half * 32 : half * 32 + R]
            v_down[:, at] = piece[half * 32 + R : half * 32 + 2 * R]
            q_up[:, at] = piece[4 * R + half * R : 5 * R + half * R]
    for h in range(KVH):
        v_up[:, h * 128 : h * 128 + 128] = pieces[2 * h, 6 * R : PIECE].astype(F32) + pieces[
            2 * h + 1, 6 * R : PIECE
        ].astype(F32)


def final(pieces):
    return pl.pallas_call(
        final_kernel,
        out_shape=(
            jax.ShapeDtypeStruct((R, D), F32),
            jax.ShapeDtypeStruct((R, H * DH), F32),
            jax.ShapeDtypeStruct((R, D), F32),
            jax.ShapeDtypeStruct((R, KVH * DH), F32),
        ),
        in_specs=[VMEM],
        out_specs=(VMEM,) * 4,
        compiler_params=params(24),
        name="final",
    )(pieces)


def exchange(array, axes):
    return lax.all_to_all(array, axes, 0, 0, tiled=True)


def body(
    features,
    queries,
    keys,
    values,
    grad_out,
    lengths,
    placement,
    query_down,
    query_up,
    value_down,
    value_up,
):
    packed = pack(
        placement[0], lengths, features[0], queries[0], keys[0], values[0], grad_out[0], query_down.T, value_down.T
    )
    recv = exchange(packed, "ctx")
    out, ups = attention(placement[0], lengths, recv, query_up, value_up)
    back = exchange(out, "ctx")
    parts = exchange(down(back, features[0]), "ctx")
    parts = exchange(chain_sum(parts, ups), "dp")
    grad_query, grad_key, grad_value = unpack(back)
    pieces = exchange(all_sum(parts), "ctx")
    q_down, q_up, v_down, v_up = final(pieces)
    return (grad_query[None], grad_key[None], grad_value[None], q_down.T, q_up, v_down.T, v_up)


def solution(mesh):
    rows = P("dp", "ctx", None)
    return jax.shard_map(
        body,
        mesh=mesh,
        in_specs=(rows,) * 5 + (P("dp"), P("dp", None)) + (P(),) * 4,
        out_specs=(rows,) * 3 + (P(),) * 4,
        check_vma=False,
    )
```
